512 devices in a mesh: seq: 64 (over y, z), rep: 8 (over x, core).
Axes of the slice: x: 4, y: 4, z: 16, core: 2. Of those that a mesh axis runs over, the one named last changes fastest.
Arguments:
- q_lin: bfloat16 [8, 8192, 4096], P('rep', 'seq'), may hold values from -90 to 90, as said below
- k_lin: bfloat16 [8, 8192, 512], P('rep', 'seq'), may hold values from -4 to 4
- value_projection: bfloat16 [8, 8192, 512], P('rep', 'seq'), may hold values from -6 to 6
- grad_out: bfloat16 [8, 8192, 4096], P('rep', 'seq'), may hold values from -6 to 6
- q_bias: float32 [4096], replicated, may hold values from -3 to 3
- block_lists: int32 [32, 64, 2], replicated, may hold values from 0 to 63, as said below
- block_counts: int32 [32, 64], replicated, may hold values from 1 to 2, as said below
Outputs:
- dq: bfloat16 [8, 8192, 4096], P('rep', 'seq')
- dk: bfloat16 [8, 8192, 512], P('rep', 'seq')
- dv: bfloat16 [8, 8192, 512], P('rep', 'seq')
- dbq: float32 [4096], replicated
The draws below stay inside these ranges and needn't reach their ends.
Inputs may be any that keep to these rules, and one draw needn't show every extreme that they name: `q_lin`: in the shown and hidden draws alike the entries stay within the stated range. `block_lists`: entry 0 of every list is the query block itself; the 2 entries of a list are distinct; entries past block_counts are ignored. `block_counts`: some head has 2 for every query block.
All inputs are finite; a program needn't handle non-finite values.
Results may differ from the reference program's by a relative error of at most 0.008.
Values may be sent and summed in bfloat16 or wider, within the bound.
No kernel may reach another device: no remote copies, remote signals or barrier semaphores. Data moves between devices by JAX's collectives and lax.ppermute only.
A program may use at most 128 MiB of HBM per device.

```python
import jax
import jax.numpy as jnp
from jax import lax

QUERY_HEADS = 32
KEY_VALUE_HEADS = 4
HEAD_WIDTH = 128
BLOCK = 128
SEL = 2
SEQUENCE_LENGTH = 8192
BATCH_COUNT = 8
QBLOCKS = 64
GROUP_SIZE = 8


def query_key_pair(key):
    base = jax.random.fold_in(key, 11)
    key_query, key_random_keys = jax.random.split(base, 2)
    gathered_keys = jnp.clip(jax.random.normal(key_random_keys, (BATCH_COUNT, SEQUENCE_LENGTH, KEY_VALUE_HEADS, HEAD_WIDTH), jnp.float32), -4.0, 4.0)
    query_rows = jnp.clip(jax.random.normal(key_query, (BATCH_COUNT, SEQUENCE_LENGTH, QUERY_HEADS, HEAD_WIDTH), jnp.float32), -4.0, 4.0)
    return (query_rows.reshape(BATCH_COUNT, SEQUENCE_LENGTH, QUERY_HEADS * HEAD_WIDTH), gathered_keys.reshape(BATCH_COUNT, SEQUENCE_LENGTH, KEY_VALUE_HEADS * HEAD_WIDTH))


def draw_q_lin(key, part):
    return query_key_pair(key)[0].astype(jnp.bfloat16)


def draw_k_lin(key, part):
    return query_key_pair(key)[1].astype(jnp.bfloat16)


def mask_tables(key):
    base = jax.random.fold_in(key, 7)
    key_levels, key_heavy, key_shift, key_picks = jax.random.split(base, 4)
    levels = jax.random.randint(key_levels, (QUERY_HEADS,), 1, SEL + 1)
    heavy = jax.random.randint(key_heavy, (), 0, QUERY_HEADS)
    shifts = jax.random.randint(key_shift, (QUERY_HEADS, QBLOCKS), 0, 2)
    counts = jnp.clip(levels[:, None] - shifts, 1, SEL)
    counts = counts.at[heavy].set(SEL)
    row_keys = jax.random.split(key_picks, QUERY_HEADS * QBLOCKS)
    others = jax.vmap(lambda row_key: jax.random.permutation(row_key, QBLOCKS - 1)[:SEL - 1])(row_keys)
    others = others.reshape(QUERY_HEADS, QBLOCKS, SEL - 1)
    own = jnp.broadcast_to(jnp.arange(QBLOCKS, dtype=jnp.int32)[None, :, None], (QUERY_HEADS, QBLOCKS, 1))
    others = (own + 1 + others) % QBLOCKS
    chosen = jnp.concatenate([own, others.astype(jnp.int32)], axis=2)
    return (chosen.astype(jnp.int32), counts.astype(jnp.int32))


def draw_block_lists(key, part):
    return mask_tables(key)[0]


def draw_block_counts(key, part):
    return mask_tables(key)[1]


def block_scale(own_key, extent, shards, low, top_value):
    def one(position, parts):
        draws = jax.random.uniform(jax.random.fold_in(jax.random.fold_in(own_key, 6), position), (parts,), jnp.float32, low / len(shards), top_value / len(shards))
        return jnp.repeat(jnp.exp(draws), extent[position] // parts).reshape((-1,) + (1,) * (len(extent) - position - 1))

    factor_of = one(*shards[0])
    for cut in shards[1:]:
        factor_of = factor_of * one(*cut)
    return factor_of


def normal_values(key, dims, width, most, cuts=(), kind=jnp.bfloat16):
    gain = block_scale(key, dims, cuts, -0.22, 0.18) if cuts else 1.0
    drawn = jax.random.normal(key, dims, jnp.float32) * width * gain
    return jnp.minimum(jnp.maximum(drawn, -most), most).astype(kind)


def setup_inputs(seed: int = 0) -> dict:
    keys = jax.random.split(jax.random.key(seed), 8)
    return {
        "q_lin": draw_q_lin(jax.random.fold_in(keys[7], 71), 0),
        "k_lin": draw_k_lin(jax.random.fold_in(keys[7], 71), 0),
        "value_projection": normal_values(keys[2], (BATCH_COUNT, SEQUENCE_LENGTH, KEY_VALUE_HEADS * HEAD_WIDTH), 1.0, 6.0, ((0, 8), (1, 64))),
        "grad_out": normal_values(keys[3], (BATCH_COUNT, SEQUENCE_LENGTH, QUERY_HEADS * HEAD_WIDTH), 1.0, 6.0, ((0, 8), (1, 64))),
        "q_bias": normal_values(keys[4], (QUERY_HEADS * HEAD_WIDTH,), 0.5, 3.0, (), jnp.float32),
        "block_lists": draw_block_lists(jax.random.fold_in(keys[7], 71), 0),
        "block_counts": draw_block_counts(jax.random.fold_in(keys[7], 71), 0),
    }


def rounded(values_in):
    return lax.optimization_barrier(values_in.astype(jnp.bfloat16)).astype(jnp.float32)


def head_pass(query_rows, key_rows, value_rows, grads, chosen, counts):
    scaling = HEAD_WIDTH ** -0.5
    q_blocks = query_rows.reshape(QBLOCKS, BLOCK, HEAD_WIDTH).astype(jnp.float32)
    key_sel = key_rows.reshape(QBLOCKS, BLOCK, HEAD_WIDTH)[chosen].reshape(QBLOCKS, SEL * BLOCK, HEAD_WIDTH).astype(jnp.float32)
    value_sel = value_rows.reshape(QBLOCKS, BLOCK, HEAD_WIDTH)[chosen].reshape(QBLOCKS, SEL * BLOCK, HEAD_WIDTH).astype(jnp.float32)
    g_blocks = grads.reshape(QBLOCKS, BLOCK, HEAD_WIDTH).astype(jnp.float32)
    active = jnp.repeat(jnp.arange(SEL, dtype=jnp.int32)[None, :] < counts[:, None], BLOCK, axis=1)
    scores = jnp.einsum("qrd,qkd->qrk", q_blocks, key_sel) * scaling
    scores = jnp.where(active[:, None, :], scores, -1.0e30)
    weights = jax.nn.softmax(scores, axis=-1)
    weights_half = rounded(weights)
    attn_out = jnp.einsum("qrk,qkd->qrd", weights_half, value_sel)
    row_dots = jnp.sum(g_blocks * attn_out, axis=-1)
    weight_grads = jnp.einsum("qrd,qkd->qrk", g_blocks, value_sel)
    score_grads = rounded(weights * (weight_grads - row_dots[..., None]))
    grad_q = scaling * jnp.einsum("qrk,qkd->qrd", score_grads, key_sel)
    dk_sel = scaling * jnp.einsum("qrk,qrd->qkd", score_grads, q_blocks)
    dv_sel = jnp.einsum("qrk,qrd->qkd", weights_half, g_blocks)
    empty = jnp.zeros((QBLOCKS, BLOCK, HEAD_WIDTH), jnp.float32)
    key_gradient = empty.at[chosen].add(dk_sel.reshape(QBLOCKS, SEL, BLOCK, HEAD_WIDTH))
    value_gradient = empty.at[chosen].add(dv_sel.reshape(QBLOCKS, SEL, BLOCK, HEAD_WIDTH))
    return grad_q.reshape(SEQUENCE_LENGTH, HEAD_WIDTH), key_gradient.reshape(SEQUENCE_LENGTH, HEAD_WIDTH), value_gradient.reshape(SEQUENCE_LENGTH, HEAD_WIDTH)


def reference(q_lin, k_lin, value_projection, grad_out, q_bias, block_lists, block_counts):
    query_rows = (q_lin.astype(jnp.float32) + q_bias).astype(jnp.bfloat16)
    group_of = jnp.arange(QUERY_HEADS, dtype=jnp.int32) // GROUP_SIZE

    def per_sequence(members):
        q_seq, key_sequence, value_sequence, g_seq = members
        q_heads = jnp.transpose(q_seq.reshape(SEQUENCE_LENGTH, QUERY_HEADS, HEAD_WIDTH), (1, 0, 2))
        g_heads = jnp.transpose(g_seq.reshape(SEQUENCE_LENGTH, QUERY_HEADS, HEAD_WIDTH), (1, 0, 2))
        key_head_rows = jnp.transpose(key_sequence.reshape(SEQUENCE_LENGTH, KEY_VALUE_HEADS, HEAD_WIDTH), (1, 0, 2))
        value_head_rows = jnp.transpose(value_sequence.reshape(SEQUENCE_LENGTH, KEY_VALUE_HEADS, HEAD_WIDTH), (1, 0, 2))

        def per_head(inner):
            q_one, g_one, chosen, counts, group = inner
            key_rows = lax.dynamic_index_in_dim(key_head_rows, group, 0, keepdims=False)
            value_rows = lax.dynamic_index_in_dim(value_head_rows, group, 0, keepdims=False)
            return head_pass(q_one, key_rows, value_rows, g_one, chosen, counts)

        grad_q, key_gradient, value_gradient = lax.map(per_head, (q_heads, g_heads, block_lists, block_counts, group_of))
        bias_part = jnp.sum(grad_q, axis=1)
        dq_seq = jnp.transpose(grad_q, (1, 0, 2)).reshape(SEQUENCE_LENGTH, QUERY_HEADS * HEAD_WIDTH).astype(jnp.bfloat16)
        key_gradient_sequence = jnp.sum(key_gradient.reshape(KEY_VALUE_HEADS, GROUP_SIZE, SEQUENCE_LENGTH, HEAD_WIDTH), axis=1)
        value_gradient_sequence = jnp.sum(value_gradient.reshape(KEY_VALUE_HEADS, GROUP_SIZE, SEQUENCE_LENGTH, HEAD_WIDTH), axis=1)
        key_gradient_sequence = jnp.transpose(key_gradient_sequence, (1, 0, 2)).reshape(SEQUENCE_LENGTH, KEY_VALUE_HEADS * HEAD_WIDTH).astype(jnp.bfloat16)
        value_gradient_sequence = jnp.transpose(value_gradient_sequence, (1, 0, 2)).reshape(SEQUENCE_LENGTH, KEY_VALUE_HEADS * HEAD_WIDTH).astype(jnp.bfloat16)
        return dq_seq, key_gradient_sequence, value_gradient_sequence, bias_part

    dq, dk, dv, bias_parts = lax.map(per_sequence, (query_rows, k_lin, value_projection, grad_out))
    return dq, dk, dv, jnp.sum(bias_parts, axis=0).reshape(QUERY_HEADS * HEAD_WIDTH)
```

```python
import functools

import jax
import jax.numpy as jnp
from jax import lax
from jax.experimental import pallas as pl
from jax.experimental.pallas import tpu as pltpu
from jax.sharding import Mesh
from jax.sharding import PartitionSpec as P

SEQ = ("y", "z")
REP = ("x", "core")
HEAD = 128
BLOCK = 128
GROUP = 8
NEG = -1e30


def dot(a, b, ca, cb):
    return lax.dot_general(a, b, (((ca,), (cb,)), ((), ())), preferred_element_type=jnp.float32)


def attend_kernel(
    other_ref, count_ref, own_ref, kv_ref, q_ref, g_ref, dq_ref, dkv_ref, dbq_ref, acc_ref
):
    step = pl.program_id(0)
    scaling = HEAD**-0.5

    @pl.when(step == 0)
    def _():
        acc_ref[...] = jnp.zeros_like(acc_ref)
        dbq_ref[...] = jnp.zeros_like(dbq_ref)

    own = own_ref[step]
    key_own = kv_ref[own, 0]
    value_own = kv_ref[own, 1]
    key_position = lax.broadcasted_iota(jnp.int32, (2 * BLOCK, 1), 0)
    dk_own = jnp.zeros((BLOCK, HEAD), jnp.float32)
    dv_own = jnp.zeros((BLOCK, HEAD), jnp.float32)
    for h in range(GROUP):
        other = other_ref[h, step]
        limit = count_ref[h, step] * BLOCK
        cols = slice(h * HEAD, (h + 1) * HEAD)
        q = q_ref[0, :, cols]
        g = g_ref[0, :, cols]
        keys = jnp.concatenate([key_own, kv_ref[other, 0]], axis=0)
        values = jnp.concatenate([value_own, kv_ref[other, 1]], axis=0)
        scores = dot(keys, q, 1, 1) * scaling
        scores = jnp.where(key_position < limit, scores, NEG)
        top = jnp.max(scores, axis=0, keepdims=True)
        raised = jnp.exp(scores - top)
        weights = raised / jnp.sum(raised, axis=0, keepdims=True)
        weights_half = weights.astype(jnp.bfloat16)
        weight_grads = dot(values, g, 1, 1)
        row_dots = jnp.sum(weights_half.astype(jnp.float32) * weight_grads, axis=0, keepdims=True)
        score_grads = (weights * (weight_grads - row_dots)).astype(jnp.bfloat16)
        grad_q = scaling * dot(score_grads, keys, 0, 0)
        dk = scaling * dot(score_grads, q, 1, 0)
        dv = dot(weights_half, g, 1, 0)
        dq_ref[0, :, cols] = grad_q.astype(jnp.bfloat16)
        dbq_ref[h : h + 1, :] += jnp.sum(grad_q, axis=0, keepdims=True)
        dk_own += dk[:BLOCK]
        dv_own += dv[:BLOCK]
        acc_ref[other, 0] += dk[BLOCK:]
        acc_ref[other, 1] += dv[BLOCK:]
    acc_ref[own, 0] += dk_own
    acc_ref[own, 1] += dv_own

    @pl.when(step == pl.num_programs(0) - 1)
    def _():
        @pl.loop(0, acc_ref.shape[0])
        def _(n):
            dkv_ref[n] = acc_ref[n].astype(jnp.bfloat16)


def attend(other, counts, own, kv, q, g):
    blocks, rows, width = q.shape
    tiles = kv.shape[0]
    per_block = pl.BlockSpec((1, rows, width), lambda i, *_: (i, 0, 0))
    whole = pl.BlockSpec(kv.shape, lambda i, *_: (0, 0, 0, 0))
    return pl.pallas_call(
        attend_kernel,
        grid_spec=pltpu.PrefetchScalarGridSpec(
            num_scalar_prefetch=3,
            grid=(blocks,),
            in_specs=[whole, per_block, per_block],
            out_specs=[per_block, whole, pl.BlockSpec((GROUP, HEAD), lambda i, *_: (0, 0))],
            scratch_shapes=[pltpu.VMEM(kv.shape, jnp.float32)],
        ),
        out_shape=[
            jax.ShapeDtypeStruct(q.shape, jnp.bfloat16),
            jax.ShapeDtypeStruct(kv.shape, jnp.bfloat16),
            jax.ShapeDtypeStruct((GROUP, HEAD), jnp.float32),
        ],
        compiler_params=pltpu.CompilerParams(
            dimension_semantics=("arbitrary",), vmem_limit_bytes=48 * 1024 * 1024
        ),
        cost_estimate=pl.CostEstimate(
            flops=14 * blocks * GROUP * rows * 2 * BLOCK * HEAD,
            bytes_accessed=14 * 1024 * 1024,
            transcendentals=blocks * GROUP * rows * 2 * BLOCK,
        ),
    )(other, counts, own, kv, q, g)


def by_group(x, groups):
    rows, width = x.shape
    return jnp.transpose(x.reshape(rows, groups, width // groups), (1, 0, 2))


def side_by_side(x):
    groups, rows, width = x.shape
    return jnp.transpose(x, (1, 0, 2)).reshape(rows, groups * width)


def body(q_lin, k_lin, value_projection, grad_out, q_bias, block_lists, block_counts):
    my_y = lax.axis_index("y")
    my_z = lax.axis_index("z")
    y_size = lax.axis_size("y")
    z_size = lax.axis_size("z")
    groups = y_size
    exchange = functools.partial(
        lax.all_to_all, axis_name="y", split_axis=0, concat_axis=0, tiled=True
    )

    kv_mine = jnp.stack([by_group(k_lin[0], groups), by_group(value_projection[0], groups)], axis=1)
    kv_head = exchange(kv_mine)
    kv_all = lax.all_gather(kv_head, "z", axis=0, tiled=True)

    query_rows = (q_lin[0].astype(jnp.float32) + q_bias).astype(jnp.bfloat16)
    qg = jnp.stack([by_group(query_rows, groups), by_group(grad_out[0], groups)], axis=1)
    qg, kv_head = lax.optimization_barrier((qg, kv_head))
    got = exchange(qg)
    got_q, got_g = got[:, 0], got[:, 1]

    mine = (GROUP, y_size, z_size)
    lists = lax.dynamic_slice_in_dim(block_lists[:, :, 1], my_y * GROUP, GROUP, axis=0)
    lists = lax.dynamic_index_in_dim(lists.reshape(mine), my_z, 2, keepdims=False)
    counts = lax.dynamic_slice_in_dim(block_counts, my_y * GROUP, GROUP, axis=0)
    counts = lax.dynamic_index_in_dim(counts.reshape(mine), my_z, 2, keepdims=False)
    other = lists % z_size * y_size + lists // z_size
    own = my_z * y_size + jnp.arange(y_size, dtype=jnp.int32)

    dq_head, dkv_all, dbq_part = attend(other, counts, own, kv_all, got_q, got_g)

    dkv_head = lax.psum_scatter(dkv_all, "z", scatter_dimension=0, tiled=True)
    dq_out = side_by_side(exchange(dq_head))[None]
    dbq_z = jnp.sum(lax.all_gather(dbq_part, "z", axis=0), axis=0)
    dbq_head = jnp.sum(lax.all_gather(dbq_z, REP, axis=0), axis=0)
    dbq_out = lax.all_gather(dbq_head, "y", axis=0, tiled=True).reshape(-1)

    dkv_mine = exchange(dkv_head)
    dk_out = side_by_side(dkv_mine[:, 0])[None]
    dv_out = side_by_side(dkv_mine[:, 1])[None]
    return dq_out, dk_out, dv_out, dbq_out


def solution(mesh):
    torus = Mesh(mesh.devices.reshape(4, 16, 4, 2), ("y", "z", "x", "core"))
    split = P(REP, SEQ, None)
    return jax.shard_map(
        body,
        mesh=torus,
        in_specs=(split, split, split, split, P(), P(), P()),
        out_specs=(split, split, split, P()),
        check_vma=False,
    )
```

```python
import functools

import jax
import jax.numpy as jnp
from jax import lax
from jax.experimental import pallas as pl
from jax.experimental.pallas import tpu as pltpu
from jax.sharding import Mesh
from jax.sharding import PartitionSpec as P

SEQ = ("y", "z")
REP = ("x", "core")
HEAD = 128
BLOCK = 128
GROUP = 8
NEG = -1e30


def dot(a, b, ca, cb):
    return lax.dot_general(a, b, (((ca,), (cb,)), ((), ())), preferred_element_type=jnp.float32)


def attend_kernel(
    other_ref, count_ref, own_ref, kv_ref, qg_ref, dq_ref, dkv_ref, dbq_ref, acc_ref
):
    step = pl.program_id(0)
    scaling = HEAD**-0.5

    @pl.when(step == 0)
    def _():
        acc_ref[...] = jnp.zeros_like(acc_ref)
        dbq_ref[...] = jnp.zeros_like(dbq_ref)

    heads = range(GROUP)
    cols = [slice(h * HEAD, (h + 1) * HEAD) for h in heads]
    own = own_ref[step]
    others = [other_ref[h, step] for h in heads]
    q = [qg_ref[0, 0, :, c] for c in cols]
    g = [qg_ref[0, 1, :, c] for c in cols]
    q_all = jnp.concatenate(q, axis=0)
    g_all = jnp.concatenate(g, axis=0)
    key_own = kv_ref[own, 0]
    value_own = kv_ref[own, 1]
    key_other = [kv_ref[n, 0] for n in others]
    value_other = [kv_ref[n, 1] for n in others]

    scores_own = dot(key_own, q_all, 1, 1)
    scores_other = jnp.concatenate([dot(key_other[h], q[h], 1, 1) for h in heads], axis=1)
    closed = jnp.concatenate(
        [jnp.full((1, BLOCK), jnp.where(count_ref[h, step] > 1, 0.0, NEG)) for h in heads], axis=1
    )
    scores_other = scores_other + closed
    top = jnp.maximum(
        jnp.max(scores_own, axis=0, keepdims=True), jnp.max(scores_other, axis=0, keepdims=True)
    )
    raised_own = jnp.exp((scores_own - top) * scaling)
    raised_other = jnp.exp((scores_other - top) * scaling)
    share = 1.0 / (
        jnp.sum(raised_own, axis=0, keepdims=True) + jnp.sum(raised_other, axis=0, keepdims=True)
    )
    weights_own = raised_own * share
    weights_other = raised_other * share
    half_own = weights_own.astype(jnp.bfloat16)
    half_other = weights_other.astype(jnp.bfloat16)
    wg_own = dot(value_own, g_all, 1, 1)
    wg_other = jnp.concatenate([dot(value_other[h], g[h], 1, 1) for h in heads], axis=1)
    row_dots = jnp.sum(half_own.astype(jnp.float32) * wg_own, axis=0, keepdims=True) + jnp.sum(
        half_other.astype(jnp.float32) * wg_other, axis=0, keepdims=True
    )
    sg_own = (weights_own * (wg_own - row_dots)).astype(jnp.bfloat16)
    sg_other = (weights_other * (wg_other - row_dots)).astype(jnp.bfloat16)
    dk_own = dot(sg_own, q_all, 1, 0)
    dv_own = dot(half_own, g_all, 1, 0)
    sums = []
    for h in heads:
        grad_q = scaling * dot(
            jnp.concatenate([sg_own[:, cols[h]], sg_other[:, cols[h]]], axis=0),
            jnp.concatenate([key_own, key_other[h]], axis=0),
            0,
            0,
        )
        dq_ref[0, :, cols[h]] = grad_q.astype(jnp.bfloat16)
        sums.append(jnp.sum(grad_q, axis=0, keepdims=True))
    dbq_ref[...] += jnp.concatenate(sums, axis=0)
    dk_other = [dot(sg_other[:, cols[h]], q[h], 1, 0) for h in heads]
    dv_other = [dot(half_other[:, cols[h]], g[h], 1, 0) for h in heads]
    acc_ref[own, 0] += dk_own
    acc_ref[own, 1] += dv_own
    for h in heads:
        acc_ref[others[h], 0] += dk_other[h]
        acc_ref[others[h], 1] += dv_other[h]

    @pl.when(step == pl.num_programs(0) - 1)
    def _():
        @pl.loop(0, acc_ref.shape[0])
        def _(n):
            dkv_ref[n, 0] = (acc_ref[n, 0] * scaling).astype(jnp.bfloat16)
            dkv_ref[n, 1] = acc_ref[n, 1].astype(jnp.bfloat16)


def attend(other, counts, own, kv, qg):
    blocks, _, rows, width = qg.shape
    whole = pl.BlockSpec(kv.shape, lambda i, *_: (0, 0, 0, 0))
    return pl.pallas_call(
        attend_kernel,
        grid_spec=pltpu.PrefetchScalarGridSpec(
            num_scalar_prefetch=3,
            grid=(blocks,),
            in_specs=[whole, pl.BlockSpec((1, 2, rows, width), lambda i, *_: (i, 0, 0, 0))],
            out_specs=[
                pl.BlockSpec((1, rows, width), lambda i, *_: (i, 0, 0)),
                whole,
                pl.BlockSpec((GROUP, HEAD), lambda i, *_: (0, 0)),
            ],
            scratch_shapes=[pltpu.VMEM(kv.shape, jnp.float32)],
        ),
        out_shape=[
            jax.ShapeDtypeStruct((blocks, rows, width), jnp.bfloat16),
            jax.ShapeDtypeStruct(kv.shape, jnp.bfloat16),
            jax.ShapeDtypeStruct((GROUP, HEAD), jnp.float32),
        ],
        compiler_params=pltpu.CompilerParams(
            dimension_semantics=("arbitrary",), vmem_limit_bytes=48 * 1024 * 1024
        ),
        cost_estimate=pl.CostEstimate(
            flops=10 * blocks * GROUP * rows * 2 * BLOCK * HEAD,
            bytes_accessed=12 * 1024 * 1024,
            transcendentals=blocks * GROUP * rows * 2 * BLOCK,
        ),
    )(other, counts, own, kv, qg)


def split_kernel(k_ref, v_ref, out_ref):
    for n in range(out_ref.shape[0]):
        cols = slice(n * HEAD, (n + 1) * HEAD)
        out_ref[n, 0] = k_ref[:, cols]
        out_ref[n, 1] = v_ref[:, cols]


def split_heads(k, v, groups):
    return pl.pallas_call(
        split_kernel, out_shape=jax.ShapeDtypeStruct((groups, 2, BLOCK, HEAD), k.dtype)
    )(k, v)


def join_kernel(x_ref, dk_ref, dv_ref, dbq_ref):
    for n in range(x_ref.shape[0]):
        cols = slice(n * HEAD, (n + 1) * HEAD)
        dk_ref[:, cols] = x_ref[n, :BLOCK]
        dv_ref[:, cols] = x_ref[n, BLOCK : 2 * BLOCK]
        pieces = [
            x_ref[n, 2 * BLOCK + 16 * p : 2 * BLOCK + 16 * (p + 1)].astype(jnp.float32)
            for p in range(3)
        ]
        dbq_ref[n] = (pieces[0] + (pieces[1] + pieces[2]))[:GROUP]


def join_heads(x):
    groups = x.shape[0]
    flat = jax.ShapeDtypeStruct((BLOCK, groups * HEAD), jnp.bfloat16)
    return pl.pallas_call(
        join_kernel,
        out_shape=[flat, flat, jax.ShapeDtypeStruct((groups, GROUP, HEAD), jnp.float32)],
    )(x)


def pack_kernel(dkv_ref, dbq_ref, out_ref):
    rest = jnp.sum(dbq_ref[...], axis=0)
    pieces = []
    for _ in range(3):
        piece = rest.astype(jnp.bfloat16)
        rest = rest - piece.astype(jnp.float32)
        pieces.append(jnp.concatenate([piece, jnp.zeros_like(piece)], axis=0))
    for n in range(out_ref.shape[0]):
        out_ref[n, :BLOCK] = dkv_ref[n, 0]
        out_ref[n, BLOCK : 2 * BLOCK] = dkv_ref[n, 1]
        for p in range(3):
            out_ref[n, 2 * BLOCK + 16 * p : 2 * BLOCK + 16 * (p + 1)] = pieces[p]


def pack(dkv, dbq):
    return pl.pallas_call(
        pack_kernel,
        out_shape=jax.ShapeDtypeStruct((dkv.shape[0], 2 * BLOCK + 48, HEAD), jnp.bfloat16),
    )(dkv, dbq)


def by_group(x, groups):
    rows, width = x.shape
    return jnp.transpose(x.reshape(rows, groups, width // groups), (1, 0, 2))


def side_by_side(x):
    groups, rows, width = x.shape
    return jnp.transpose(x, (1, 0, 2)).reshape(rows, groups * width)


def body(q_lin, k_lin, value_projection, grad_out, q_bias, block_lists, block_counts):
    my_y = lax.axis_index("y")
    my_z = lax.axis_index("z")
    y_size = lax.axis_size("y")
    z_size = lax.axis_size("z")
    groups = y_size
    exchange = functools.partial(
        lax.all_to_all, axis_name="y", split_axis=0, concat_axis=0, tiled=True
    )

    kv_head = exchange(split_heads(k_lin[0], value_projection[0], groups))
    kv_all = lax.all_gather(kv_head, "z", axis=0, tiled=True)

    query_rows = (q_lin[0].astype(jnp.float32) + q_bias).astype(jnp.bfloat16)
    qg = jnp.stack([by_group(query_rows, groups), by_group(grad_out[0], groups)], axis=1)
    got = exchange(qg)

    mine = (GROUP, y_size, z_size)
    lists = lax.dynamic_slice_in_dim(block_lists[:, :, 1], my_y * GROUP, GROUP, axis=0)
    lists = lax.dynamic_index_in_dim(lists.reshape(mine), my_z, 2, keepdims=False)
    counts = lax.dynamic_slice_in_dim(block_counts, my_y * GROUP, GROUP, axis=0)
    counts = lax.dynamic_index_in_dim(counts.reshape(mine), my_z, 2, keepdims=False)
    other = lists % z_size * y_size + lists // z_size
    own = my_z * y_size + jnp.arange(y_size, dtype=jnp.int32)

    dq_head, dkv_all, dbq_part = attend(other, counts, own, kv_all, got)

    dkv_head = lax.psum_scatter(dkv_all, "z", scatter_dimension=0, tiled=True)
    dq_out = side_by_side(exchange(dq_head))[None]
    dbq_z = jnp.sum(lax.all_gather(dbq_part, "z", axis=0), axis=0)
    dbq_rep = lax.all_gather(dbq_z, REP, axis=0)
    dk_out, dv_out, dbq_out = join_heads(exchange(pack(dkv_head, dbq_rep)))
    dk_out, dv_out, dbq_out = dk_out[None], dv_out[None], dbq_out.reshape(-1)
    return dq_out, dk_out, dv_out, dbq_out


def solution(mesh):
    torus = Mesh(mesh.devices.reshape(4, 16, 4, 2), ("y", "z", "x", "core"))
    split = P(REP, SEQ, None)
    return jax.shard_map(
        body,
        mesh=torus,
        in_specs=(split, split, split, split, P(), P(), P()),
        out_specs=(split, split, split, P()),
        check_vma=False,
    )
```

```python
import functools

import jax
import jax.numpy as jnp
from jax import lax
from jax.experimental import pallas as pl
from jax.experimental.pallas import tpu as pltpu
from jax.sharding import Mesh
from jax.sharding import PartitionSpec as P

SEQ = ("y", "z")
REP = ("x", "core")
HEAD = 128
BLOCK = 128
GROUP = 8
NEG = -1e30
CHUNKS = 4
SMALL = pltpu.CompilerParams(vmem_limit_bytes=8 * 1024 * 1024)


def dot(a, b, ca, cb):
    return lax.dot_general(a, b, (((ca,), (cb,)), ((), ())), preferred_element_type=jnp.float32)


def attend_kernel(
    other_ref, count_ref, own_ref, kv_hbm, qg_ref, dq_ref, dkv_hbm, dbq_ref, kv_ref, acc_ref, sems
):
    step = pl.program_id(0)
    scaling = HEAD**-0.5
    tiles = kv_ref.shape[0]
    chunk = tiles // CHUNKS
    parts = [pl.ds(n * chunk, chunk) for n in range(CHUNKS)]

    @pl.when(step == 0)
    def _():
        loads = [
            pltpu.make_async_copy(kv_hbm.at[part], kv_ref.at[part], sems.at[n])
            for n, part in enumerate(parts)
        ]
        for load in loads:
            load.start()
        acc_ref[...] = jnp.zeros_like(acc_ref)
        dbq_ref[...] = jnp.zeros_like(dbq_ref)
        for load in loads:
            load.wait()

    heads = range(GROUP)
    cols = [slice(h * HEAD, (h + 1) * HEAD) for h in heads]
    own = own_ref[step]
    others = [other_ref[h, step] for h in heads]
    q = [qg_ref[0, 0, :, c] for c in cols]
    g = [qg_ref[0, 1, :, c] for c in cols]
    q_all = jnp.concatenate(q, axis=0)
    g_all = jnp.concatenate(g, axis=0)
    key_own = kv_ref[own, 0]
    value_own = kv_ref[own, 1]
    key_other = [kv_ref[n, 0] for n in others]
    value_other = [kv_ref[n, 1] for n in others]

    scores_own = dot(key_own, q_all, 1, 1)
    scores_other = jnp.concatenate([dot(key_other[h], q[h], 1, 1) for h in heads], axis=1)
    closed = jnp.concatenate(
        [jnp.full((1, BLOCK), jnp.where(count_ref[h, step] > 1, 0.0, NEG)) for h in heads], axis=1
    )
    scores_other = scores_other + closed
    top = jnp.maximum(
        jnp.max(scores_own, axis=0, keepdims=True), jnp.max(scores_other, axis=0, keepdims=True)
    )
    raised_own = jnp.exp((scores_own - top) * scaling)
    raised_other = jnp.exp((scores_other - top) * scaling)
    share = 1.0 / (
        jnp.sum(raised_own, axis=0, keepdims=True) + jnp.sum(raised_other, axis=0, keepdims=True)
    )
    weights_own = raised_own * share
    weights_other = raised_other * share
    half_own = weights_own.astype(jnp.bfloat16)
    half_other = weights_other.astype(jnp.bfloat16)
    wg_own = dot(value_own, g_all, 1, 1)
    wg_other = jnp.concatenate([dot(value_other[h], g[h], 1, 1) for h in heads], axis=1)
    row_dots = jnp.sum(half_own.astype(jnp.float32) * wg_own, axis=0, keepdims=True) + jnp.sum(
        half_other.astype(jnp.float32) * wg_other, axis=0, keepdims=True
    )
    sg_own = (weights_own * (wg_own - row_dots)).astype(jnp.bfloat16)
    sg_other = (weights_other * (wg_other - row_dots)).astype(jnp.bfloat16)
    dk_own = dot(sg_own, q_all, 1, 0)
    dv_own = dot(half_own, g_all, 1, 0)
    sums = []
    for h in heads:
        grad_q = scaling * dot(
            jnp.concatenate([sg_own[:, cols[h]], sg_other[:, cols[h]]], axis=0),
            jnp.concatenate([key_own, key_other[h]], axis=0),
            0,
            0,
        )
        dq_ref[0, :, cols[h]] = grad_q.astype(jnp.bfloat16)
        sums.append(jnp.sum(grad_q, axis=0, keepdims=True))
    dbq_ref[...] += jnp.concatenate(sums, axis=0)
    dk_other = [dot(sg_other[:, cols[h]], q[h], 1, 0) for h in heads]
    dv_other = [dot(half_other[:, cols[h]], g[h], 1, 0) for h in heads]
    acc_ref[own, 0] += dk_own
    acc_ref[own, 1] += dv_own
    for h in heads:
        acc_ref[others[h], 0] += dk_other[h]
        acc_ref[others[h], 1] += dv_other[h]

    @pl.when(step == pl.num_programs(0) - 1)
    def _():
        stores = []
        for n, part in enumerate(parts):

            @pl.loop(n * chunk, (n + 1) * chunk)
            def _(tile):
                kv_ref[tile, 0] = (acc_ref[tile, 0] * scaling).astype(jnp.bfloat16)
                kv_ref[tile, 1] = acc_ref[tile, 1].astype(jnp.bfloat16)

            store = pltpu.make_async_copy(kv_ref.at[part], dkv_hbm.at[part], sems.at[n])
            store.start()
            stores.append(store)
        for store in stores:
            store.wait()


def attend(other, counts, own, kv, qg):
    blocks, _, rows, width = qg.shape
    return pl.pallas_call(
        attend_kernel,
        grid_spec=pltpu.PrefetchScalarGridSpec(
            num_scalar_prefetch=3,
            grid=(blocks,),
            in_specs=[
                pl.BlockSpec(memory_space=pl.ANY),
                pl.BlockSpec((1, 2, rows, width), lambda i, *_: (i, 0, 0, 0)),
            ],
            out_specs=[
                pl.BlockSpec((1, rows, width), lambda i, *_: (i, 0, 0)),
                pl.BlockSpec(memory_space=pl.ANY),
                pl.BlockSpec((GROUP, HEAD), lambda i, *_: (0, 0)),
            ],
            scratch_shapes=[
                pltpu.VMEM(kv.shape, jnp.bfloat16),
                pltpu.VMEM(kv.shape, jnp.float32),
                pltpu.SemaphoreType.DMA((CHUNKS,)),
            ],
        ),
        out_shape=[
            jax.ShapeDtypeStruct((blocks, rows, width), jnp.bfloat16),
            jax.ShapeDtypeStruct(kv.shape, jnp.bfloat16),
            jax.ShapeDtypeStruct((GROUP, HEAD), jnp.float32),
        ],
        compiler_params=pltpu.CompilerParams(
            dimension_semantics=("arbitrary",), vmem_limit_bytes=60 * 1024 * 1024
        ),
        cost_estimate=pl.CostEstimate(
            flops=10 * blocks * GROUP * rows * 2 * BLOCK * HEAD,
            bytes_accessed=12 * 1024 * 1024,
            transcendentals=blocks * GROUP * rows * 2 * BLOCK,
        ),
    )(other, counts, own, kv, qg)


def split_kernel(k_ref, v_ref, out_ref):
    for n in range(out_ref.shape[0]):
        cols = slice(n * HEAD, (n + 1) * HEAD)
        out_ref[n, 0] = k_ref[:, cols]
        out_ref[n, 1] = v_ref[:, cols]


def split_heads(k, v, groups):
    return pl.pallas_call(
        split_kernel,
        compiler_params=SMALL,
        out_shape=jax.ShapeDtypeStruct((groups, 2, BLOCK, HEAD), k.dtype),
    )(k, v)


def join_kernel(x_any, dk_ref, dv_ref, dbq_ref, x_ref, sem):
    load = pltpu.make_async_copy(x_any, x_ref, sem)
    load.start()
    load.wait()
    for n in range(x_ref.shape[0]):
        cols = slice(n * HEAD, (n + 1) * HEAD)
        dk_ref[:, cols] = x_ref[n, :BLOCK]
        dv_ref[:, cols] = x_ref[n, BLOCK : 2 * BLOCK]
        pieces = [
            x_ref[n, 2 * BLOCK + 16 * p : 2 * BLOCK + 16 * (p + 1)].astype(jnp.float32)
            for p in range(3)
        ]
        dbq_ref[n] = (pieces[0] + (pieces[1] + pieces[2]))[:GROUP]


def join_heads(x):
    groups = x.shape[0]
    flat = jax.ShapeDtypeStruct((BLOCK, groups * HEAD), jnp.bfloat16)
    return pl.pallas_call(
        join_kernel,
        compiler_params=SMALL,
        in_specs=[pl.BlockSpec(memory_space=pl.ANY)],
        scratch_shapes=[pltpu.VMEM(x.shape, x.dtype), pltpu.SemaphoreType.DMA],
        out_shape=[flat, flat, jax.ShapeDtypeStruct((groups, GROUP, HEAD), jnp.float32)],
    )(x)


def pack_kernel(dkv_ref, dbq_ref, out_ref):
    rest = jnp.sum(dbq_ref[...], axis=0)
    pieces = []
    for _ in range(3):
        piece = rest.astype(jnp.bfloat16)
        rest = rest - piece.astype(jnp.float32)
        pieces.append(jnp.concatenate([piece, jnp.zeros_like(piece)], axis=0))
    for n in range(out_ref.shape[0]):
        out_ref[n, :BLOCK] = dkv_ref[n, 0]
        out_ref[n, BLOCK : 2 * BLOCK] = dkv_ref[n, 1]
        for p in range(3):
            out_ref[n, 2 * BLOCK + 16 * p : 2 * BLOCK + 16 * (p + 1)] = pieces[p]


def pack(dkv, dbq):
    return pl.pallas_call(
        pack_kernel,
        compiler_params=SMALL,
        out_shape=jax.ShapeDtypeStruct((dkv.shape[0], 2 * BLOCK + 48, HEAD), jnp.bfloat16),
    )(dkv, dbq)


def by_group(x, groups):
    rows, width = x.shape
    return jnp.transpose(x.reshape(rows, groups, width // groups), (1, 0, 2))


def side_by_side(x):
    groups, rows, width = x.shape
    return jnp.transpose(x, (1, 0, 2)).reshape(rows, groups * width)


def body(q_lin, k_lin, value_projection, grad_out, q_bias, block_lists, block_counts):
    my_y = lax.axis_index("y")
    my_z = lax.axis_index("z")
    y_size = lax.axis_size("y")
    z_size = lax.axis_size("z")
    groups = y_size
    exchange = functools.partial(
        lax.all_to_all, axis_name="y", split_axis=0, concat_axis=0, tiled=True
    )

    kv_head = exchange(split_heads(k_lin[0], value_projection[0], groups))
    kv_all = lax.all_gather(kv_head, "z", axis=0, tiled=True)

    query_rows = (q_lin[0].astype(jnp.float32) + q_bias).astype(jnp.bfloat16)
    qg = jnp.stack([by_group(query_rows, groups), by_group(grad_out[0], groups)], axis=1)
    got = exchange(qg)

    mine = (GROUP, y_size, z_size)
    lists = lax.dynamic_slice_in_dim(block_lists[:, :, 1], my_y * GROUP, GROUP, axis=0)
    lists = lax.dynamic_index_in_dim(lists.reshape(mine), my_z, 2, keepdims=False)
    counts = lax.dynamic_slice_in_dim(block_counts, my_y * GROUP, GROUP, axis=0)
    counts = lax.dynamic_index_in_dim(counts.reshape(mine), my_z, 2, keepdims=False)
    other = lists % z_size * y_size + lists // z_size
    own = my_z * y_size + jnp.arange(y_size, dtype=jnp.int32)

    dq_head, dkv_all, dbq_part = attend(other, counts, own, kv_all, got)

    dkv_head = lax.psum_scatter(dkv_all, "z", scatter_dimension=0, tiled=True)
    dq_out = side_by_side(exchange(dq_head))[None]
    dbq_z = jnp.sum(lax.all_gather(dbq_part, "z", axis=0), axis=0)
    dbq_rep = lax.all_gather(dbq_z, REP, axis=0)
    dk_out, dv_out, dbq_out = join_heads(exchange(pack(dkv_head, dbq_rep)))
    dk_out, dv_out, dbq_out = dk_out[None], dv_out[None], dbq_out.reshape(-1)
    return dq_out, dk_out, dv_out, dbq_out


def solution(mesh):
    torus = Mesh(mesh.devices.reshape(4, 16, 4, 2), ("y", "z", "x", "core"))
    split = P(REP, SEQ, None)
    return jax.shard_map(
        body,
        mesh=torus,
        in_specs=(split, split, split, split, P(), P(), P()),
        out_specs=(split, split, split, P()),
        check_vma=False,
    )
```

```python
import functools

import jax
import jax.numpy as jnp
from jax import lax
from jax.experimental import pallas as pl
from jax.experimental.pallas import tpu as pltpu
from jax.sharding import Mesh
from jax.sharding import PartitionSpec as P

SEQ = ("y", "z")
REP = ("x", "core")
HEAD = 128
BLOCK = 128
GROUP = 8
NEG = -1e30
SCALING = HEAD**-0.5
COLS = [slice(h * HEAD, (h + 1) * HEAD) for h in range(GROUP)]
CHUNKS = 4
SMALL = pltpu.CompilerParams(vmem_limit_bytes=8 * 1024 * 1024)


def dot(a, b, ca, cb):
    return lax.dot_general(a, b, (((ca,), (cb,)), ((), ())), preferred_element_type=jnp.float32)


def side(parts):
    return jnp.concatenate(parts, axis=1)


def own_kernel(kv_ref, qg_ref, raised_ref, wg_ref, stats_ref):
    q_all = jnp.concatenate([qg_ref[0, 0, :, c] for c in COLS], axis=0)
    g_all = jnp.concatenate([qg_ref[0, 1, :, c] for c in COLS], axis=0)
    scores = dot(kv_ref[0, 0], q_all, 1, 1)
    top = jnp.max(scores, axis=0, keepdims=True)
    raised = jnp.exp((scores - top) * SCALING)
    raised_ref[0] = raised
    wg_ref[0] = dot(kv_ref[0, 1], g_all, 1, 1)
    stats_ref[0] = jnp.zeros_like(stats_ref[0])
    stats_ref[0, 0:1, :] = top
    stats_ref[0, 1:2, :] = jnp.sum(raised, axis=0, keepdims=True)


def own_part(kv_head, qg):
    blocks, _, rows, width = qg.shape
    square = pl.BlockSpec((1, BLOCK, width), lambda i: (i, 0, 0))
    return pl.pallas_call(
        own_kernel,
        grid=(blocks,),
        in_specs=[
            pl.BlockSpec((1, 2, BLOCK, HEAD), lambda i: (i, 0, 0, 0)),
            pl.BlockSpec((1, 2, rows, width), lambda i: (i, 0, 0, 0)),
        ],
        out_specs=[square, square, pl.BlockSpec((1, 8, width), lambda i: (i, 0, 0))],
        out_shape=[
            jax.ShapeDtypeStruct((blocks, BLOCK, width), jnp.float32),
            jax.ShapeDtypeStruct((blocks, BLOCK, width), jnp.float32),
            jax.ShapeDtypeStruct((blocks, 8, width), jnp.float32),
        ],
        compiler_params=pltpu.CompilerParams(vmem_limit_bytes=32 * 1024 * 1024),
        cost_estimate=pl.CostEstimate(
            flops=4 * blocks * BLOCK * width * HEAD,
            bytes_accessed=7 * 1024 * 1024,
            transcendentals=blocks * BLOCK * width,
        ),
    )(kv_head, qg)


def key_kernel(
    other_ref,
    count_ref,
    own_ref,
    kv_hbm,
    qg_ref,
    raised_ref,
    wg_ref,
    stats_ref,
    dkv_hbm,
    sg_ref,
    kv_ref,
    acc_ref,
    sems,
):
    step = pl.program_id(0)
    chunk = kv_ref.shape[0] // CHUNKS
    parts = [pl.ds(n * chunk, chunk) for n in range(CHUNKS)]

    @pl.when(step == 0)
    def _():
        loads = [
            pltpu.make_async_copy(kv_hbm.at[part], kv_ref.at[part], sems.at[n])
            for n, part in enumerate(parts)
        ]
        for load in loads:
            load.start()
        acc_ref[...] = jnp.zeros_like(acc_ref)
        for load in loads:
            load.wait()

    heads = range(GROUP)
    own = own_ref[step]
    others = [other_ref[h, step] for h in heads]
    q = [qg_ref[0, 0, :, c] for c in COLS]
    g = [qg_ref[0, 1, :, c] for c in COLS]
    closed = side(
        [jnp.full((1, BLOCK), jnp.where(count_ref[h, step] > 1, 0.0, NEG)) for h in heads]
    )
    scores = side([dot(kv_ref[others[h], 0], q[h], 1, 1) for h in heads]) + closed
    wg_other = side([dot(kv_ref[others[h], 1], g[h], 1, 1) for h in heads])
    top_own = stats_ref[0, 0:1, :]
    top = jnp.maximum(top_own, jnp.max(scores, axis=0, keepdims=True))
    raised = jnp.exp((scores - top) * SCALING)
    lower = jnp.exp((top_own - top) * SCALING)
    share = 1.0 / (stats_ref[0, 1:2, :] * lower + jnp.sum(raised, axis=0, keepdims=True))
    weights_own = raised_ref[0] * (lower * share)
    weights_other = raised * share
    half_own = weights_own.astype(jnp.bfloat16)
    half_other = weights_other.astype(jnp.bfloat16)
    wg_own = wg_ref[0]
    row_dots = jnp.sum(
        half_own.astype(jnp.float32) * wg_own + half_other.astype(jnp.float32) * wg_other,
        axis=0,
        keepdims=True,
    )
    sg_own = (weights_own * (wg_own - row_dots)).astype(jnp.bfloat16)
    sg_other = (weights_other * (wg_other - row_dots)).astype(jnp.bfloat16)
    sg_ref[0, 0] = sg_own
    sg_ref[0, 1] = sg_other
    dk_own = dot(sg_own, jnp.concatenate(q, axis=0), 1, 0)
    dv_own = dot(half_own, jnp.concatenate(g, axis=0), 1, 0)
    dk_other = [dot(sg_other[:, COLS[h]], q[h], 1, 0) for h in heads]
    dv_other = [dot(half_other[:, COLS[h]], g[h], 1, 0) for h in heads]
    acc_ref[own, 0] += dk_own
    acc_ref[own, 1] += dv_own
    for h in heads:
        acc_ref[others[h], 0] += dk_other[h]
        acc_ref[others[h], 1] += dv_other[h]

    @pl.when(step == pl.num_programs(0) - 1)
    def _():
        stores = []
        for n, part in enumerate(parts):

            @pl.loop(n * chunk, (n + 1) * chunk)
            def _(tile):
                kv_ref[tile, 0] = (acc_ref[tile, 0] * SCALING).astype(jnp.bfloat16)
                kv_ref[tile, 1] = acc_ref[tile, 1].astype(jnp.bfloat16)

            store = pltpu.make_async_copy(kv_ref.at[part], dkv_hbm.at[part], sems.at[n])
            store.start()
            stores.append(store)
        for store in stores:
            store.wait()


def key_part(other, counts, own, kv, qg, raised, wg, stats):
    blocks, _, rows, width = qg.shape
    square = pl.BlockSpec((1, BLOCK, width), lambda i, *_: (i, 0, 0))
    double = pl.BlockSpec((1, 2, BLOCK, width), lambda i, *_: (i, 0, 0, 0))
    return pl.pallas_call(
        key_kernel,
        grid_spec=pltpu.PrefetchScalarGridSpec(
            num_scalar_prefetch=3,
            grid=(blocks,),
            in_specs=[
                pl.BlockSpec(memory_space=pl.ANY),
                double,
                square,
                square,
                pl.BlockSpec((1, 8, width), lambda i, *_: (i, 0, 0)),
            ],
            out_specs=[pl.BlockSpec(memory_space=pl.ANY), double],
            scratch_shapes=[
                pltpu.VMEM(kv.shape, jnp.bfloat16),
                pltpu.VMEM(kv.shape, jnp.float32),
                pltpu.SemaphoreType.DMA((CHUNKS,)),
            ],
        ),
        out_shape=[
            jax.ShapeDtypeStruct(kv.shape, jnp.bfloat16),
            jax.ShapeDtypeStruct((blocks, 2, BLOCK, width), jnp.bfloat16),
        ],
        compiler_params=pltpu.CompilerParams(
            dimension_semantics=("arbitrary",), vmem_limit_bytes=60 * 1024 * 1024
        ),
        cost_estimate=pl.CostEstimate(
            flops=12 * blocks * BLOCK * width * HEAD,
            bytes_accessed=16 * 1024 * 1024,
            transcendentals=blocks * BLOCK * width,
        ),
    )(other, counts, own, kv, qg, raised, wg, stats)


def query_kernel(other_ref, kv_ref, own_ref, sg_ref, dq_ref, dbq_ref):
    step = pl.program_id(0)

    @pl.when(step == 0)
    def _():
        dbq_ref[...] = jnp.zeros_like(dbq_ref)

    sums = []
    for h in range(GROUP):
        grads = jnp.concatenate([sg_ref[0, 0, :, COLS[h]], sg_ref[0, 1, :, COLS[h]]], axis=0)
        keys = jnp.concatenate([own_ref[0, 0], kv_ref[other_ref[h, step], 0]], axis=0)
        grad_q = SCALING * dot(grads, keys, 0, 0)
        dq_ref[0, :, COLS[h]] = grad_q.astype(jnp.bfloat16)
        sums.append(jnp.sum(grad_q, axis=0, keepdims=True))
    dbq_ref[...] += jnp.concatenate(sums, axis=0)


def query_part(other, kv, kv_head, sg):
    blocks, _, rows, width = sg.shape
    return pl.pallas_call(
        query_kernel,
        grid_spec=pltpu.PrefetchScalarGridSpec(
            num_scalar_prefetch=1,
            grid=(blocks,),
            in_specs=[
                pl.BlockSpec(kv.shape, lambda i, *_: (0, 0, 0, 0)),
                pl.BlockSpec((1, 2, BLOCK, HEAD), lambda i, *_: (i, 0, 0, 0)),
                pl.BlockSpec((1, 2, BLOCK, width), lambda i, *_: (i, 0, 0, 0)),
            ],
            out_specs=[
                pl.BlockSpec((1, rows, width), lambda i, *_: (i, 0, 0)),
                pl.BlockSpec((GROUP, HEAD), lambda i, *_: (0, 0)),
            ],
        ),
        out_shape=[
            jax.ShapeDtypeStruct((blocks, rows, width), jnp.bfloat16),
            jax.ShapeDtypeStruct((GROUP, HEAD), jnp.float32),
        ],
        compiler_params=pltpu.CompilerParams(
            dimension_semantics=("arbitrary",), vmem_limit_bytes=32 * 1024 * 1024
        ),
        cost_estimate=pl.CostEstimate(
            flops=4 * blocks * BLOCK * width * HEAD,
            bytes_accessed=7 * 1024 * 1024,
            transcendentals=0,
        ),
    )(other, kv, kv_head, sg)


def split_kernel(k_ref, v_ref, out_ref):
    for n in range(out_ref.shape[0]):
        cols = slice(n * HEAD, (n + 1) * HEAD)
        out_ref[n, 0] = k_ref[:, cols]
        out_ref[n, 1] = v_ref[:, cols]


def split_heads(k, v, groups):
    return pl.pallas_call(
        split_kernel,
        compiler_params=SMALL,
        out_shape=jax.ShapeDtypeStruct((groups, 2, BLOCK, HEAD), k.dtype),
    )(k, v)


def join_kernel(x_any, dk_ref, dv_ref, x_ref, sem):
    load = pltpu.make_async_copy(x_any, x_ref, sem)
    load.start()
    load.wait()
    for n in range(x_ref.shape[0]):
        cols = slice(n * HEAD, (n + 1) * HEAD)
        dk_ref[:, cols] = x_ref[n, 0]
        dv_ref[:, cols] = x_ref[n, 1]


def join_heads(x):
    flat = jax.ShapeDtypeStruct((BLOCK, x.shape[0] * HEAD), jnp.bfloat16)
    return pl.pallas_call(
        join_kernel,
        compiler_params=SMALL,
        in_specs=[pl.BlockSpec(memory_space=pl.ANY)],
        scratch_shapes=[pltpu.VMEM(x.shape, x.dtype), pltpu.SemaphoreType.DMA],
        out_shape=[flat, flat],
    )(x)


def pieces_kernel(dbq_ref, out_ref):
    rest = jnp.sum(dbq_ref[...], axis=0)
    row = lax.broadcasted_iota(jnp.int32, (16, HEAD), 0)
    blocks = [jnp.zeros((16, HEAD), jnp.float32)] * GROUP
    for p in range(3):
        piece = rest.astype(jnp.bfloat16).astype(jnp.float32)
        rest = rest - piece
        blocks = [jnp.where(row == p, piece[h : h + 1], blocks[h]) for h in range(GROUP)]
    for h in range(GROUP):
        out_ref[:, COLS[h]] = blocks[h].astype(jnp.bfloat16)


def pieces(dbq):
    return pl.pallas_call(
        pieces_kernel,
        compiler_params=SMALL,
        out_shape=jax.ShapeDtypeStruct((16, GROUP * HEAD), jnp.bfloat16),
    )(dbq)


def by_group(x, groups):
    rows, width = x.shape
    return jnp.transpose(x.reshape(rows, groups, width // groups), (1, 0, 2))


def side_by_side(x):
    groups, rows, width = x.shape
    return jnp.transpose(x, (1, 0, 2)).reshape(rows, groups * width)


def body(q_lin, k_lin, value_projection, grad_out, q_bias, block_lists, block_counts):
    my_y = lax.axis_index("y")
    my_z = lax.axis_index("z")
    y_size = lax.axis_size("y")
    z_size = lax.axis_size("z")
    groups = y_size
    exchange = functools.partial(
        lax.all_to_all, axis_name="y", split_axis=0, concat_axis=0, tiled=True
    )

    kv_head = exchange(split_heads(k_lin[0], value_projection[0], groups))
    kv_all = lax.all_gather(kv_head, "z", axis=0, tiled=True)

    query_rows = (q_lin[0].astype(jnp.float32) + q_bias).astype(jnp.bfloat16)
    qg = jnp.stack([by_group(query_rows, groups), by_group(grad_out[0], groups)], axis=1)
    got = exchange(qg)

    mine = (GROUP, y_size, z_size)
    lists = lax.dynamic_slice_in_dim(block_lists[:, :, 1], my_y * GROUP, GROUP, axis=0)
    lists = lax.dynamic_index_in_dim(lists.reshape(mine), my_z, 2, keepdims=False)
    counts = lax.dynamic_slice_in_dim(block_counts, my_y * GROUP, GROUP, axis=0)
    counts = lax.dynamic_index_in_dim(counts.reshape(mine), my_z, 2, keepdims=False)
    other = lists % z_size * y_size + lists // z_size
    own = my_z * y_size + jnp.arange(y_size, dtype=jnp.int32)

    raised, wg, stats = own_part(kv_head, got)
    dkv_all, score_grads = key_part(other, counts, own, kv_all, got, raised, wg, stats)
    dkv_head = lax.psum_scatter(dkv_all, "z", scatter_dimension=0, tiled=True)

    dq_head, dbq_part = query_part(other, kv_all, kv_head, score_grads)
    dbq_z = jnp.sum(lax.all_gather(dbq_part, "z", axis=0), axis=0)
    dbq_rows = pieces(lax.all_gather(dbq_z, REP, axis=0))
    dbq_rows = jnp.broadcast_to(dbq_rows, (groups,) + dbq_rows.shape)
    back = exchange(jnp.concatenate([dq_head, dbq_rows], axis=1))
    dq_out = side_by_side(back[:, :BLOCK])[None]
    dbq_out = jnp.sum(back[:, BLOCK : BLOCK + 3].astype(jnp.float32), axis=1).reshape(-1)

    dk_out, dv_out = join_heads(exchange(dkv_head))
    dk_out, dv_out = dk_out[None], dv_out[None]
    return dq_out, dk_out, dv_out, dbq_out


def solution(mesh):
    torus = Mesh(mesh.devices.reshape(4, 16, 4, 2), ("y", "z", "x", "core"))
    split = P(REP, SEQ, None)
    return jax.shard_map(
        body,
        mesh=torus,
        in_specs=(split, split, split, split, P(), P(), P()),
        out_specs=(split, split, split, P()),
        check_vma=False,
    )
```
